128 devices in a mesh: region: 8 (over y, core), dev: 16 (over x, z).
Axes of the slice: x: 4, y: 4, z: 4, core: 2. Of those that a mesh axis runs over, the one named last changes fastest.
Arguments:
- a_vals: bfloat16 [16384, 16, 4096], P(('region', 'dev')), may hold values from -0.75 to 0.75
- a_cols: int32 [16384, 16], P(('region', 'dev')), may hold values from 0 to 2047, as said below
- p_vals: bfloat16 [16384, 2, 4096], P(('region', 'dev')), may hold values from -0.75 to 0.75
- send_slot: int32 [16384, 2, 16, 2], P(('region', 'dev')), may hold values from 0 to 511, as said below
- recv_slot: int32 [128, 512], P(('region', 'dev')), may hold values from 0 to 63
Outputs:
- coarse: float32 [8192, 4096], P(('region', 'dev'))
The draws below stay inside these ranges and needn't reach their ends.
Inputs may be any that keep to these rules, and one draw needn't show every extreme that they name: `a_cols`: each row's first entry is the row itself; every entry names a row of the same device or of the devices just before and after it along dev in the same region. `send_slot`: most terms go to owners in the row's own region; some slots may stay empty.
All inputs are finite; a program needn't handle non-finite values.
Results may differ from the reference program's by a relative error of at most 0.0029.
Values may be sent and summed in bfloat16 or wider, within the bound.
A program may use at most 256 MiB of HBM per device.

```python
import jax
import jax.numpy as jnp
from jax import lax

B = 64
K = 16
KP = 2
CAP = 4
SLOTS = 64
ROW_DEV = 128
GROUP_ROWS = 2048
FINE_ROWS = 16384
OWNERS = 128
BUCKETS = 512
N_DEV = 16


def draw_a_cols(key, part):
    key = jax.random.fold_in(key, 11)
    rows_all = jnp.arange(FINE_ROWS, dtype=jnp.int32)
    local_row = rows_all % GROUP_ROWS
    device_row = local_row // ROW_DEV
    lowest = jnp.maximum(device_row - 1, 0) * ROW_DEV
    highest = jnp.minimum((device_row + 2) * ROW_DEV, GROUP_ROWS)
    picks = jax.random.randint(key, (FINE_ROWS, K), 0, 24 * ROW_DEV)
    columns = lowest[:, None] + picks % (highest - lowest)[:, None]
    columns = columns.at[:, 0].set(local_row)
    return columns.astype(jnp.int32)


def draw_send_slot(key, part):
    key = jax.random.fold_in(key, 23)
    key_pick, key_far, key_near, key_place = jax.random.split(key, 4)
    shape_full = (FINE_ROWS, KP, K, KP)
    home_region = (jnp.arange(FINE_ROWS, dtype=jnp.int32) // GROUP_ROWS)[:, None, None, None]
    per_group = GROUP_ROWS // ROW_DEV
    chooser = jax.random.randint(key_pick, shape_full, 0, 4)
    far_owner = jax.random.randint(key_far, shape_full, 0, OWNERS)
    near_owner = home_region * per_group + jax.random.randint(key_near, shape_full, 0, per_group)
    owner = jnp.where(chooser < 3, near_owner, far_owner)
    place = jax.random.randint(key_place, shape_full, 0, CAP)
    values = (owner * CAP + place).reshape(-1)
    values = values.at[0].set(0).at[-1].set(BUCKETS - 1)
    return values.reshape(shape_full).astype(jnp.int32)


def draw_recv_slot(key, part):
    key = jax.random.fold_in(key, 37)
    values = jax.random.randint(key, (OWNERS * BUCKETS,), 0, SLOTS)
    values = values.at[0].set(0).at[-1].set(SLOTS - 1)
    return values.reshape(OWNERS, BUCKETS).astype(jnp.int32)


def steps_of(rng, shape, shards, low, high):
    level = 1.0
    for axis_at, shards_of in shards:
        heights = jax.random.uniform(jax.random.fold_in(jax.random.fold_in(rng, 6), axis_at), (shards_of,), jnp.float32, low / len(shards), high / len(shards))
        level = level * jnp.repeat(jnp.exp(heights), shape[axis_at] // shards_of).reshape((-1,) + (1,) * (len(shape) - 1 - axis_at))
    return level


def scatter_about(key, dims, scale, bound, pieces=(), kind=jnp.bfloat16):
    loudness = steps_of(key, dims, pieces, -0.22, 0.18) if pieces else 1.0
    array = jax.random.normal(key, dims, jnp.float32) * scale * loudness
    return jnp.minimum(jnp.maximum(array, -bound), bound).astype(kind)


def setup_inputs(seed: int = 0) -> dict:
    key_list = jax.random.split(jax.random.key(seed), 6)
    return {
        "a_vals": scatter_about(key_list[0], (FINE_ROWS, K, B * B), B ** -0.5, 0.75, ((0, 128),)),
        "a_cols": draw_a_cols(jax.random.fold_in(key_list[5], 71), 0),
        "p_vals": scatter_about(key_list[2], (FINE_ROWS, KP, B * B), B ** -0.5, 0.75, ((0, 128),)),
        "send_slot": draw_send_slot(jax.random.fold_in(key_list[5], 71), 0),
        "recv_slot": draw_recv_slot(jax.random.fold_in(key_list[5], 71), 0),
    }


def reference(a_vals, a_cols, p_vals, send_slot, recv_slot):
    tile_area = B * B
    a_split = a_vals.reshape(OWNERS, ROW_DEV, K, B, B)
    p_split = p_vals.reshape(OWNERS, ROW_DEV, KP, B, B)
    col_split = a_cols.reshape(OWNERS, ROW_DEV, K)
    slot_split = send_slot.reshape(OWNERS, ROW_DEV * KP * K * KP)
    bucket_ids = jnp.arange(BUCKETS, dtype=jnp.int32)
    bucket_owner = bucket_ids // CAP
    bucket_place = bucket_ids % CAP

    def one_device(result, device):
        region_start = ((device // N_DEV) * GROUP_ROWS).astype(jnp.int32)
        group_p = lax.dynamic_slice_in_dim(p_vals, region_start, GROUP_ROWS, 0)
        right_rows = jnp.take(group_p, col_split[device], axis=0).reshape(ROW_DEV, K, KP, B, B)
        inner_tiles = jnp.einsum("rkab,rkpbc->rkpac", a_split[device].astype(jnp.float32), right_rows.astype(jnp.float32)).astype(jnp.bfloat16)
        tile_terms = jnp.einsum("rqba,rkpbc->rqkpac", p_split[device].astype(jnp.float32), inner_tiles.astype(jnp.float32))
        totals = jax.ops.segment_sum(tile_terms.reshape(-1, tile_area), slot_split[device], num_segments=BUCKETS)
        target = bucket_owner * SLOTS + recv_slot[bucket_owner, device * CAP + bucket_place]
        return result.at[target].add(totals), None

    start = jnp.zeros((OWNERS * SLOTS, tile_area), jnp.float32)
    result, _ = lax.scan(one_device, start, jnp.arange(OWNERS, dtype=jnp.int32))
    return result
```

```python
import functools

import jax
import jax.numpy as jnp
from jax import lax
from jax.experimental import pallas as pl
from jax.experimental.pallas import tpu as pltpu
from jax.sharding import PartitionSpec as P

B = 64
CAP = 4
SLOTS = 64
HALF = B // 2
WIDE = 2 * B
ROWS_STEP = 8
BATCH = 4


def left_lanes(shape):
    return lax.broadcasted_iota(jnp.int32, shape, len(shape) - 1) < B


def spread(tile):
    other = jnp.concatenate([tile[:, B:], tile[:, :B]], axis=1)
    left = left_lanes(tile.shape)
    zero = jnp.zeros_like(tile)
    return jnp.concatenate(
        [
            jnp.where(left, tile, zero),
            jnp.where(left, other, zero),
            jnp.where(left, zero, other),
            jnp.where(left, zero, tile),
        ],
        axis=0,
    )


def terms_kernel(a_blocks, cols, slots, a_ref, p_ref, low, own, high, out, right, inner, acc0, acc1, acc2, acc3, sems):
    step = pl.program_id(0)
    rows = own.shape[0]
    accs = ((acc0, acc1), (acc2, acc3))
    copies = [
        pltpu.make_async_copy(source, right.at[pl.ds(n * rows, rows)], sems.at[n])
        for n, source in enumerate((low, own, high))
    ]

    @pl.when(step == 0)
    def _():
        for copy in copies:
            copy.start()

        def clear(n, _):
            for pair in accs:
                for acc in pair:
                    acc[n] = jnp.zeros((HALF, WIDE), jnp.float32)
            return 0

        lax.fori_loop(0, out.shape[0], clear, 0, unroll=4)
        for copy in copies:
            copy.wait()

    def inner_tiles(row):
        first = (step * ROWS_STEP + row) * a_blocks
        for k in range(a_blocks):
            tile = spread(a_ref[row * a_blocks + k])
            lhs = right[pl.ds(2 * cols[first + k], 2)].reshape(2 * HALF, WIDE)
            inner[row, pl.ds(k * B, B)] = jnp.dot(
                lhs, tile, preferred_element_type=jnp.float32
            ).astype(jnp.bfloat16)

    def add_terms(row):
        first = (step * ROWS_STEP + row) * a_blocks
        weights = jnp.concatenate([spread(p_ref[2 * row]), spread(p_ref[2 * row + 1])], axis=1)
        for start in range(0, a_blocks, BATCH):
            terms = jnp.dot(
                inner[row, pl.ds(start * B, BATCH * B)], weights, preferred_element_type=jnp.float32
            )
            for k in range(BATCH):
                at = (first + start + k) * 4
                where = [[slots[at + 2 * q + p] for p in range(2)] for q in range(2)]
                old = [[accs[q][p][where[q][p]] for p in range(2)] for q in range(2)]
                for q in range(2):
                    for p in range(2):
                        top = k * B + p * HALF
                        part = terms[top : top + HALF, q * WIDE : (q + 1) * WIDE]
                        accs[q][p][where[q][p]] = old[q][p] + part

    for row in range(ROWS_STEP):
        inner_tiles(row)
    for row in range(ROWS_STEP):
        add_terms(row)

    @pl.when(step == pl.num_programs(0) - 1)
    def _():
        def finish(n, _):
            out[n] = ((acc0[n] + acc1[n]) + (acc2[n] + acc3[n])).astype(jnp.bfloat16)
            return 0

        lax.fori_loop(0, out.shape[0], finish, 0, unroll=4)


def bucket_sums(a_tiles, cols, slots, p_tiles, low, own, high, buckets):
    row_total = p_tiles.shape[0] // 2
    a_blocks = a_tiles.shape[0] // row_total
    return pl.pallas_call(
        functools.partial(terms_kernel, a_blocks),
        grid_spec=pltpu.PrefetchScalarGridSpec(
            num_scalar_prefetch=2,
            grid=(row_total // ROWS_STEP,),
            in_specs=[
                pl.BlockSpec((ROWS_STEP * a_blocks, HALF, WIDE), lambda i, *_: (i, 0, 0)),
                pl.BlockSpec((ROWS_STEP * 2, HALF, WIDE), lambda i, *_: (i, 0, 0)),
                pl.BlockSpec(memory_space=pl.ANY),
                pl.BlockSpec(memory_space=pl.ANY),
                pl.BlockSpec(memory_space=pl.ANY),
            ],
            out_specs=pl.BlockSpec((buckets, HALF, WIDE), lambda i, *_: (0, 0, 0)),
            scratch_shapes=[pltpu.VMEM((3 * 2 * row_total, HALF, WIDE), jnp.bfloat16)]
            + [pltpu.VMEM((ROWS_STEP, a_blocks * B, WIDE), jnp.bfloat16)]
            + [pltpu.VMEM((buckets, HALF, WIDE), jnp.float32)] * 4
            + [pltpu.SemaphoreType.DMA((3,))],
        ),
        out_shape=jax.ShapeDtypeStruct((buckets, HALF, WIDE), jnp.bfloat16),
        compiler_params=pltpu.CompilerParams(
            dimension_semantics=("arbitrary",), vmem_limit_bytes=58 * 2**20
        ),
        cost_estimate=pl.CostEstimate(
            flops=2**33, bytes_accessed=24 * 2**20, transcendentals=0
        ),
        name="terms",
    )(cols, slots, a_tiles, p_tiles, low, own, high)


def gather_kernel(places, arrived, out):
    out[...] = jnp.zeros_like(out)

    def add(n, _):
        place = places[n]
        out[place] += arrived[n].astype(jnp.float32)
        return 0

    lax.fori_loop(0, arrived.shape[0], add, 0, unroll=4)


def owner_sums(places, arrived):
    return pl.pallas_call(
        gather_kernel,
        in_specs=[
            pl.BlockSpec(memory_space=pltpu.SMEM),
            pl.BlockSpec(memory_space=pltpu.VMEM),
        ],
        out_specs=pl.BlockSpec(memory_space=pltpu.VMEM),
        out_shape=jax.ShapeDtypeStruct((SLOTS, HALF, WIDE), jnp.float32),
        compiler_params=pltpu.CompilerParams(vmem_limit_bytes=32 * 2**20),
        name="owner_sums",
    )(places, arrived)


def shards(a_vals, a_cols, p_vals, send_slot, recv_slot):
    rows, a_blocks, tile_area = a_vals.shape
    owners = lax.axis_size("region") * lax.axis_size("dev")
    buckets = owners * CAP
    count = lax.axis_size("dev")

    turned = jnp.swapaxes(p_vals.reshape(rows * 2, B, B), 1, 2).reshape(rows * 2, HALF, WIDE)
    forward = [(i, i + 1) for i in range(count - 1)]
    low = lax.ppermute(turned, "dev", forward)
    high = lax.ppermute(turned, "dev", [(t, s) for s, t in forward])

    cols = (a_cols - (lax.axis_index("dev") - 1) * rows).reshape(-1)
    slots = jnp.transpose(send_slot, (0, 2, 1, 3)).reshape(-1)
    a_tiles = jnp.transpose(
        a_vals.reshape(rows * a_blocks, B, 2, HALF), (0, 3, 2, 1)
    ).reshape(rows * a_blocks, HALF, WIDE)
    p_tiles = jnp.swapaxes(p_vals.reshape(rows * 2, 2, HALF, B), 1, 2).reshape(rows * 2, HALF, WIDE)
    totals = bucket_sums(a_tiles, cols, slots, p_tiles, low, turned, high, buckets)

    arrived = lax.all_to_all(
        totals, ("region", "dev"), split_axis=0, concat_axis=0, tiled=True
    )
    sums = owner_sums(recv_slot.reshape(-1), arrived)
    return jnp.swapaxes(sums.reshape(SLOTS, B, B), 1, 2).reshape(SLOTS, tile_area)


def solution(mesh):
    in_specs = (
        P(("region", "dev"), None, None),
        P(("region", "dev"), None),
        P(("region", "dev"), None, None),
        P(("region", "dev"), None, None, None),
        P(("region", "dev"), None),
    )
    out_specs = P(("region", "dev"), None)
    return jax.shard_map(shards, mesh=mesh, in_specs=in_specs, out_specs=out_specs, check_vma=False)
```

```python
import functools

import jax
import jax.numpy as jnp
from jax import lax
from jax.experimental import pallas as pl
from jax.experimental.pallas import tpu as pltpu
from jax.sharding import PartitionSpec as P

B = 64
CAP = 4
SLOTS = 64
HALF = B // 2
WIDE = 2 * B
ROWS_STEP = 8
BATCH = 4
PREP = 16
F32 = jnp.float32
BF16 = jnp.bfloat16


def left_lanes(shape):
    return lax.broadcasted_iota(jnp.int32, shape, len(shape) - 1) < B


def swap_lanes(tile):
    return jnp.concatenate([tile[:, B:], tile[:, :B]], axis=1)


def even_odd(first, second):
    left = left_lanes(first.shape)
    even = jnp.where(left, first, swap_lanes(second))
    odd = jnp.where(left, swap_lanes(first), second)
    return even, odd


def turn_pair(first, second, mixed, turned):
    even, odd = even_odd(first, second)
    mixed[pl.ds(0, HALF, stride=2)] = even
    mixed[pl.ds(1, HALF, stride=2)] = odd
    rows = mixed[...]
    turned[...] = jnp.concatenate([rows, rows], axis=0).T
    top = turned[pl.ds(0, B, stride=2)]
    low = turned[pl.ds(1, B, stride=2)]
    return jnp.where(left_lanes(top.shape), top, low)


def p_kernel(p_ref, plain, turned_out, flat, mixed, turned):
    def one(pair, _):
        for u in range(2):
            row = pair * 2 + u
            value = p_ref[row].astype(F32)
            for r in range(HALF):
                flat[u, pl.ds(2 * r, 2)] = value[:, r * WIDE : (r + 1) * WIDE]
            first = flat[u, pl.ds(0, HALF, stride=2)]
            second = flat[u, pl.ds(1, HALF, stride=2)]
            plain[row] = jnp.concatenate([first, second], axis=0).astype(BF16)
            turned_out[row] = turn_pair(first, second, mixed.at[u], turned.at[u]).astype(BF16)
        return 0

    lax.fori_loop(0, PREP // 2, one, 0, unroll=2)


def p_tiles_of(p_vals):
    rows = p_vals.shape[0]
    block = pl.BlockSpec((PREP, B, WIDE), lambda i: (i, 0, 0))
    return pl.pallas_call(
        p_kernel,
        grid=(rows // PREP,),
        in_specs=[pl.BlockSpec((PREP,) + p_vals.shape[1:], lambda i: (i, 0, 0))],
        out_specs=[block, block],
        out_shape=[jax.ShapeDtypeStruct((rows, B, WIDE), BF16)] * 2,
        scratch_shapes=[
            pltpu.VMEM((2, B, WIDE), F32),
            pltpu.VMEM((2, B, WIDE), F32),
            pltpu.VMEM((2, WIDE, WIDE), F32),
        ],
        name="p_tiles",
    )(p_vals)


def a_kernel(a_ref, out, flat):
    a_blocks = a_ref.shape[1]

    def one(pair, _):
        for u in range(2):
            row = pair * 2 + u
            value = a_ref[row].astype(F32)
            for half in range(a_blocks // 8):
                for r in range(HALF):
                    flat[u, pl.ds((half * HALF + r) * 8, 8)] = value[
                        half * 8 : half * 8 + 8, r * WIDE : (r + 1) * WIDE
                    ]
            for k in range(0, a_blocks, 2):
                at = (k // 8) * HALF * 8 + k % 8
                first = flat[u, pl.ds(at, HALF, stride=8)]
                second = flat[u, pl.ds(at + 1, HALF, stride=8)]
                even, odd = even_odd(first, second)
                turned = jnp.concatenate([even, odd, even, odd], axis=0).T.astype(BF16)
                out[row * a_blocks + k] = turned[:B]
                out[row * a_blocks + k + 1] = turned[B:]
        return 0

    lax.fori_loop(0, PREP // 2, one, 0)


def a_tiles_of(a_vals):
    rows, a_blocks, area = a_vals.shape
    return pl.pallas_call(
        a_kernel,
        grid=(rows // PREP,),
        in_specs=[pl.BlockSpec((PREP, a_blocks, area), lambda i: (i, 0, 0))],
        out_specs=pl.BlockSpec((PREP * a_blocks, B, WIDE), lambda i: (i, 0, 0)),
        out_shape=jax.ShapeDtypeStruct((rows * a_blocks, B, WIDE), BF16),
        scratch_shapes=[pltpu.VMEM((2, a_blocks * HALF, WIDE), F32)],
        compiler_params=pltpu.CompilerParams(vmem_limit_bytes=48 * 2**20),
        cost_estimate=pl.CostEstimate(flops=2**33, bytes_accessed=48 * 2**20, transcendentals=0),
        name="a_tiles",
    )(a_vals)


def spread(tile):
    other = swap_lanes(tile)
    left = left_lanes(tile.shape)
    zero = jnp.zeros_like(tile)
    return jnp.concatenate(
        [
            jnp.where(left, tile, zero),
            jnp.where(left, other, zero),
            jnp.where(left, zero, other),
            jnp.where(left, zero, tile),
        ],
        axis=0,
    )


def terms_kernel(a_blocks, cols, slots, a_ref, p_ref, low, own, high, out, right, inner, acc0, acc1, acc2, acc3, sems):
    step = pl.program_id(0)
    rows = own.shape[0]
    accs = ((acc0, acc1), (acc2, acc3))
    copies = [
        pltpu.make_async_copy(source, right.at[pl.ds(n * rows, rows)], sems.at[n])
        for n, source in enumerate((low, own, high))
    ]

    @pl.when(step == 0)
    def _():
        for copy in copies:
            copy.start()

        def clear(n, _):
            for pair in accs:
                for acc in pair:
                    acc[n] = jnp.zeros((HALF, WIDE), F32)
            return 0

        lax.fori_loop(0, out.shape[0], clear, 0, unroll=4)
        for copy in copies:
            copy.wait()

    left = left_lanes((B, WIDE))
    zero = jnp.zeros((B, WIDE), BF16)

    def inner_tiles(row):
        first = (step * ROWS_STEP + row) * a_blocks
        for k in range(a_blocks):
            tile = a_ref[row * a_blocks + k]
            tile = jnp.concatenate(
                [jnp.where(left, tile, zero), jnp.where(left, zero, tile)], axis=0
            )
            lhs = right[cols[first + k]]
            inner[row, pl.ds(k * B, B)] = jnp.dot(
                lhs, tile, preferred_element_type=F32
            ).astype(BF16)

    def add_terms(row):
        first = (step * ROWS_STEP + row) * a_blocks
        weights = jnp.concatenate(
            [spread(p_ref[row, pl.ds(0, HALF)]), spread(p_ref[row, pl.ds(HALF, HALF)])], axis=1
        )
        for start in range(0, a_blocks, BATCH):
            terms = jnp.dot(
                inner[row, pl.ds(start * B, BATCH * B)], weights, preferred_element_type=F32
            )
            for k in range(BATCH):
                at = (first + start + k) * 4
                where = [[slots[at + 2 * q + p] for p in range(2)] for q in range(2)]
                old = [[accs[q][p][where[q][p]] for p in range(2)] for q in range(2)]
                for q in range(2):
                    for p in range(2):
                        top = k * B + p * HALF
                        part = terms[top : top + HALF, q * WIDE : (q + 1) * WIDE]
                        accs[q][p][where[q][p]] = old[q][p] + part

    for row in range(ROWS_STEP):
        inner_tiles(row)
    for row in range(ROWS_STEP):
        add_terms(row)

    @pl.when(step == pl.num_programs(0) - 1)
    def _():
        def finish(n, _):
            out[n] = ((acc0[n] + acc1[n]) + (acc2[n] + acc3[n])).astype(BF16)
            return 0

        lax.fori_loop(0, out.shape[0], finish, 0, unroll=4)


def bucket_sums(a_tiles, cols, slots, p_tiles, low, own, high, buckets):
    row_total = p_tiles.shape[0]
    a_blocks = a_tiles.shape[0] // row_total
    return pl.pallas_call(
        functools.partial(terms_kernel, a_blocks),
        grid_spec=pltpu.PrefetchScalarGridSpec(
            num_scalar_prefetch=2,
            grid=(row_total // ROWS_STEP,),
            in_specs=[
                pl.BlockSpec((ROWS_STEP * a_blocks, B, WIDE), lambda i, *_: (i, 0, 0)),
                pl.BlockSpec((ROWS_STEP, B, WIDE), lambda i, *_: (i, 0, 0)),
                pl.BlockSpec(memory_space=pl.ANY),
                pl.BlockSpec(memory_space=pl.ANY),
                pl.BlockSpec(memory_space=pl.ANY),
            ],
            out_specs=pl.BlockSpec((buckets, HALF, WIDE), lambda i, *_: (0, 0, 0)),
            scratch_shapes=[pltpu.VMEM((3 * row_total, B, WIDE), BF16)]
            + [pltpu.VMEM((ROWS_STEP, a_blocks * B, WIDE), BF16)]
            + [pltpu.VMEM((buckets, HALF, WIDE), F32)] * 4
            + [pltpu.SemaphoreType.DMA((3,))],
        ),
        out_shape=jax.ShapeDtypeStruct((buckets, HALF, WIDE), BF16),
        compiler_params=pltpu.CompilerParams(
            dimension_semantics=("arbitrary",), vmem_limit_bytes=58 * 2**20
        ),
        cost_estimate=pl.CostEstimate(
            flops=2**33, bytes_accessed=24 * 2**20, transcendentals=0
        ),
        name="terms",
    )(cols, slots, a_tiles, p_tiles, low, own, high)


def owner_kernel(places, arrived, out, sums, mixed, turned, flat):
    sums[...] = jnp.zeros_like(sums)

    def add(n, _):
        place = places[n]
        sums[place] += arrived[n].astype(F32)
        return 0

    lax.fori_loop(0, arrived.shape[0], add, 0, unroll=8)

    def turn(group, _):
        for u in range(4):
            slot = group * 8 + 2 * u
            pair = turn_pair(sums[slot], sums[slot + 1], mixed.at[u], turned.at[u])
            for n in range(2):
                flat[pl.ds(2 * u + n, HALF, stride=8)] = pair[n * HALF : (n + 1) * HALF]
        for r in range(HALF):
            out[pl.ds(group * 8, 8), pl.ds(r * WIDE, WIDE)] = flat[pl.ds(r * 8, 8)]
        return 0

    lax.fori_loop(0, SLOTS // 8, turn, 0)


def owner_sums(places, arrived):
    return pl.pallas_call(
        owner_kernel,
        in_specs=[
            pl.BlockSpec(memory_space=pltpu.SMEM),
            pl.BlockSpec(memory_space=pltpu.VMEM),
        ],
        out_specs=pl.BlockSpec(memory_space=pltpu.VMEM),
        out_shape=jax.ShapeDtypeStruct((SLOTS, B * B), F32),
        scratch_shapes=[
            pltpu.VMEM((SLOTS, HALF, WIDE), F32),
            pltpu.VMEM((4, B, WIDE), F32),
            pltpu.VMEM((4, WIDE, WIDE), F32),
            pltpu.VMEM((8 * HALF, WIDE), F32),
        ],
        compiler_params=pltpu.CompilerParams(vmem_limit_bytes=32 * 2**20),
        name="owner_sums",
    )(places, arrived)


def shards(a_vals, a_cols, p_vals, send_slot, recv_slot):
    rows, a_blocks, tile_area = a_vals.shape
    owners = lax.axis_size("region") * lax.axis_size("dev")
    buckets = owners * CAP
    count = lax.axis_size("dev")

    plain, turned = p_tiles_of(p_vals)
    forward = [(i, i + 1) for i in range(count - 1)]
    low = lax.ppermute(turned, "dev", forward)
    high = lax.ppermute(turned, "dev", [(t, s) for s, t in forward])

    cols = (a_cols - (lax.axis_index("dev") - 1) * rows).reshape(-1)
    slots = jnp.transpose(send_slot, (0, 2, 1, 3)).reshape(-1)
    a_tiles = a_tiles_of(a_vals)
    totals = bucket_sums(a_tiles, cols, slots, plain, low, turned, high, buckets)

    arrived = lax.all_to_all(
        totals, ("region", "dev"), split_axis=0, concat_axis=0, tiled=True
    )
    return owner_sums(recv_slot.reshape(-1), arrived)


def solution(mesh):
    in_specs = (
        P(("region", "dev"), None, None),
        P(("region", "dev"), None),
        P(("region", "dev"), None, None),
        P(("region", "dev"), None, None, None),
        P(("region", "dev"), None),
    )
    out_specs = P(("region", "dev"), None)
    return jax.shard_map(shards, mesh=mesh, in_specs=in_specs, out_specs=out_specs, check_vma=False)
```

```python
import functools

import jax
import jax.numpy as jnp
from jax import lax
from jax.experimental import pallas as pl
from jax.experimental.pallas import tpu as pltpu
from jax.sharding import PartitionSpec as P

B = 64
CAP = 4
SLOTS = 64
HALF = B // 2
WIDE = 2 * B
ROWS_STEP = 8
BATCH = 4
PREP = 16
F32 = jnp.float32
BF16 = jnp.bfloat16


def left_lanes(shape):
    return lax.broadcasted_iota(jnp.int32, shape, len(shape) - 1) < B


def swap_lanes(tile):
    return jnp.concatenate([tile[:, B:], tile[:, :B]], axis=1)


def even_odd(first, second):
    left = left_lanes(first.shape)
    even = jnp.where(left, first, swap_lanes(second))
    odd = jnp.where(left, swap_lanes(first), second)
    return even, odd


def turn_pair(first, second, mixed, turned):
    even, odd = even_odd(first, second)
    mixed[pl.ds(0, HALF, stride=2)] = even
    mixed[pl.ds(1, HALF, stride=2)] = odd
    rows = mixed[...]
    turned[...] = jnp.concatenate([rows, rows], axis=0).T
    top = turned[pl.ds(0, B, stride=2)]
    low = turned[pl.ds(1, B, stride=2)]
    return jnp.where(left_lanes(top.shape), top, low)


def p_kernel(p_ref, plain, turned_out, flat, mixed, turned):
    def one(pair, _):
        for u in range(2):
            row = pair * 2 + u
            value = p_ref[row].astype(F32)
            for r in range(HALF):
                flat[u, pl.ds(2 * r, 2)] = value[:, r * WIDE : (r + 1) * WIDE]
            first = flat[u, pl.ds(0, HALF, stride=2)]
            second = flat[u, pl.ds(1, HALF, stride=2)]
            plain[row] = jnp.concatenate([first, second], axis=0).astype(BF16)
            turned_out[row] = turn_pair(first, second, mixed.at[u], turned.at[u]).astype(BF16)
        return 0

    lax.fori_loop(0, PREP // 2, one, 0, unroll=4)


def p_tiles_of(p_vals):
    rows = p_vals.shape[0]
    block = pl.BlockSpec((PREP, B, WIDE), lambda i: (i, 0, 0))
    return pl.pallas_call(
        p_kernel,
        grid=(rows // PREP,),
        in_specs=[pl.BlockSpec((PREP,) + p_vals.shape[1:], lambda i: (i, 0, 0))],
        out_specs=[block, block],
        out_shape=[jax.ShapeDtypeStruct((rows, B, WIDE), BF16)] * 2,
        scratch_shapes=[
            pltpu.VMEM((2, B, WIDE), F32),
            pltpu.VMEM((2, B, WIDE), F32),
            pltpu.VMEM((2, WIDE, WIDE), F32),
        ],
        name="p_tiles",
    )(p_vals)


def a_kernel(a_ref, out, flat):
    a_blocks = a_ref.shape[1]

    def one(pair, _):
        for u in range(2):
            row = pair * 2 + u
            value = a_ref[row].astype(F32)
            for half in range(a_blocks // 8):
                for r in range(HALF):
                    flat[u, pl.ds((half * HALF + r) * 8, 8)] = value[
                        half * 8 : half * 8 + 8, r * WIDE : (r + 1) * WIDE
                    ]
            for k in range(0, a_blocks, 2):
                at = (k // 8) * HALF * 8 + k % 8
                first = flat[u, pl.ds(at, HALF, stride=8)]
                second = flat[u, pl.ds(at + 1, HALF, stride=8)]
                even, odd = even_odd(first, second)
                turned = jnp.concatenate([even, odd, even, odd], axis=0).T.astype(BF16)
                out[row * a_blocks + k] = turned[:B]
                out[row * a_blocks + k + 1] = turned[B:]
        return 0

    lax.fori_loop(0, PREP // 2, one, 0, unroll=2)


def a_tiles_of(a_vals):
    rows, a_blocks, area = a_vals.shape
    return pl.pallas_call(
        a_kernel,
        grid=(rows // PREP,),
        in_specs=[pl.BlockSpec((PREP, a_blocks, area), lambda i: (i, 0, 0))],
        out_specs=pl.BlockSpec((PREP * a_blocks, B, WIDE), lambda i: (i, 0, 0)),
        out_shape=jax.ShapeDtypeStruct((rows * a_blocks, B, WIDE), BF16),
        scratch_shapes=[pltpu.VMEM((2, a_blocks * HALF, WIDE), F32)],
        compiler_params=pltpu.CompilerParams(vmem_limit_bytes=48 * 2**20),
        cost_estimate=pl.CostEstimate(flops=2**33, bytes_accessed=48 * 2**20, transcendentals=0),
        name="a_tiles",
    )(a_vals)


def spread(tile):
    other = swap_lanes(tile)
    left = left_lanes(tile.shape)
    zero = jnp.zeros_like(tile)
    return jnp.concatenate(
        [
            jnp.where(left, tile, zero),
            jnp.where(left, other, zero),
            jnp.where(left, zero, other),
            jnp.where(left, zero, tile),
        ],
        axis=0,
    )


def terms_kernel(a_blocks, cols, slots, a_ref, p_ref, low, own, high, out, right, inner, acc0, acc1, acc2, acc3, sems):
    step = pl.program_id(0)
    rows = own.shape[0]
    shift = (lax.axis_index("dev") - 1) * rows
    accs = ((acc0, acc1), (acc2, acc3))
    copies = [
        pltpu.make_async_copy(source, right.at[pl.ds(n * rows, rows)], sems.at[n])
        for n, source in enumerate((low, own, high))
    ]

    @pl.when(step == 0)
    def _():
        for copy in copies:
            copy.start()

        def clear(n, _):
            for pair in accs:
                for acc in pair:
                    acc[n] = jnp.zeros((HALF, WIDE), F32)
            return 0

        lax.fori_loop(0, out.shape[0], clear, 0, unroll=4)
        for copy in copies:
            copy.wait()

    left = left_lanes((B, WIDE))
    zero = jnp.zeros((B, WIDE), BF16)

    def inner_tiles(row):
        fine = step * ROWS_STEP + row
        for k in range(a_blocks):
            tile = a_ref[row * a_blocks + k]
            tile = jnp.concatenate(
                [jnp.where(left, tile, zero), jnp.where(left, zero, tile)], axis=0
            )
            lhs = right[cols[k * rows + fine] - shift]
            inner[row, pl.ds(k * B, B)] = jnp.dot(
                lhs, tile, preferred_element_type=F32
            ).astype(BF16)

    def add_terms(row):
        fine = step * ROWS_STEP + row
        weights = jnp.concatenate(
            [spread(p_ref[row, pl.ds(0, HALF)]), spread(p_ref[row, pl.ds(HALF, HALF)])], axis=1
        )
        for start in range(0, a_blocks, BATCH):
            terms = jnp.dot(
                inner[row, pl.ds(start * B, BATCH * B)], weights, preferred_element_type=F32
            )
            for k in range(BATCH):
                where = [
                    [
                        slots[((q * a_blocks + start + k) * 2 + p) * rows + fine]
                        for p in range(2)
                    ]
                    for q in range(2)
                ]
                old = [[accs[q][p][where[q][p]] for p in range(2)] for q in range(2)]
                for q in range(2):
                    for p in range(2):
                        top = k * B + p * HALF
                        part = terms[top : top + HALF, q * WIDE : (q + 1) * WIDE]
                        accs[q][p][where[q][p]] = old[q][p] + part

    for row in range(ROWS_STEP):
        inner_tiles(row)
    for row in range(ROWS_STEP):
        add_terms(row)

    @pl.when(step == pl.num_programs(0) - 1)
    def _():
        def finish(n, _):
            out[n] = ((acc0[n] + acc1[n]) + (acc2[n] + acc3[n])).astype(BF16)
            return 0

        lax.fori_loop(0, out.shape[0], finish, 0, unroll=4)


def bucket_sums(a_tiles, cols, slots, p_tiles, low, own, high, buckets):
    row_total = p_tiles.shape[0]
    a_blocks = a_tiles.shape[0] // row_total
    return pl.pallas_call(
        functools.partial(terms_kernel, a_blocks),
        grid_spec=pltpu.PrefetchScalarGridSpec(
            num_scalar_prefetch=2,
            grid=(row_total // ROWS_STEP,),
            in_specs=[
                pl.BlockSpec((ROWS_STEP * a_blocks, B, WIDE), lambda i, *_: (i, 0, 0)),
                pl.BlockSpec((ROWS_STEP, B, WIDE), lambda i, *_: (i, 0, 0)),
                pl.BlockSpec(memory_space=pl.ANY),
                pl.BlockSpec(memory_space=pl.ANY),
                pl.BlockSpec(memory_space=pl.ANY),
            ],
            out_specs=pl.BlockSpec((buckets, HALF, WIDE), lambda i, *_: (0, 0, 0)),
            scratch_shapes=[pltpu.VMEM((3 * row_total, B, WIDE), BF16)]
            + [pltpu.VMEM((ROWS_STEP, a_blocks * B, WIDE), BF16)]
            + [pltpu.VMEM((buckets, HALF, WIDE), F32)] * 4
            + [pltpu.SemaphoreType.DMA((3,))],
        ),
        out_shape=jax.ShapeDtypeStruct((buckets, HALF, WIDE), BF16),
        compiler_params=pltpu.CompilerParams(
            dimension_semantics=("arbitrary",), vmem_limit_bytes=58 * 2**20
        ),
        cost_estimate=pl.CostEstimate(
            flops=2**33, bytes_accessed=24 * 2**20, transcendentals=0
        ),
        name="terms",
    )(cols, slots, a_tiles, p_tiles, low, own, high)


def owner_kernel(places, arrived, out, sums, mixed, turned, flat):
    sums[...] = jnp.zeros_like(sums)

    def add(n, _):
        place = places[n]
        sums[place] += arrived[n].astype(F32)
        return 0

    lax.fori_loop(0, arrived.shape[0], add, 0, unroll=8)

    def turn(group, _):
        for u in range(4):
            slot = group * 8 + 2 * u
            pair = turn_pair(sums[slot], sums[slot + 1], mixed.at[u], turned.at[u])
            for n in range(2):
                flat[pl.ds(2 * u + n, HALF, stride=8)] = pair[n * HALF : (n + 1) * HALF]
        for r in range(HALF):
            out[pl.ds(group * 8, 8), pl.ds(r * WIDE, WIDE)] = flat[pl.ds(r * 8, 8)]
        return 0

    lax.fori_loop(0, SLOTS // 8, turn, 0)


def owner_sums(places, arrived):
    return pl.pallas_call(
        owner_kernel,
        in_specs=[
            pl.BlockSpec(memory_space=pltpu.SMEM),
            pl.BlockSpec(memory_space=pltpu.VMEM),
        ],
        out_specs=pl.BlockSpec(memory_space=pltpu.VMEM),
        out_shape=jax.ShapeDtypeStruct((SLOTS, B * B), F32),
        scratch_shapes=[
            pltpu.VMEM((SLOTS, HALF, WIDE), F32),
            pltpu.VMEM((4, B, WIDE), F32),
            pltpu.VMEM((4, WIDE, WIDE), F32),
            pltpu.VMEM((8 * HALF, WIDE), F32),
        ],
        compiler_params=pltpu.CompilerParams(vmem_limit_bytes=32 * 2**20),
        name="owner_sums",
    )(places, arrived)


def shards(a_vals, a_cols, p_vals, send_slot, recv_slot):
    rows, a_blocks, tile_area = a_vals.shape
    owners = lax.axis_size("region") * lax.axis_size("dev")
    buckets = owners * CAP
    count = lax.axis_size("dev")

    plain, turned = p_tiles_of(p_vals)
    forward = [(i, i + 1) for i in range(count - 1)]
    low = lax.ppermute(turned, "dev", forward)
    high = lax.ppermute(turned, "dev", [(t, s) for s, t in forward])

    cols = jnp.transpose(a_cols).reshape(-1)
    slots = jnp.transpose(send_slot, (1, 2, 3, 0)).reshape(-1)
    a_tiles = a_tiles_of(a_vals)
    totals = bucket_sums(a_tiles, cols, slots, plain, low, turned, high, buckets)

    arrived = lax.all_to_all(
        totals, ("region", "dev"), split_axis=0, concat_axis=0, tiled=True
    )
    return owner_sums(recv_slot.reshape(-1), arrived)


def solution(mesh):
    in_specs = (
        P(("region", "dev"), None, None),
        P(("region", "dev"), None),
        P(("region", "dev"), None, None),
        P(("region", "dev"), None, None, None),
        P(("region", "dev"), None),
    )
    out_specs = P(("region", "dev"), None)
    return jax.shard_map(shards, mesh=mesh, in_specs=in_specs, out_specs=out_specs, check_vma=False)
```

```python
import functools

import jax
import jax.numpy as jnp
from jax import lax
from jax.experimental import pallas as pl
from jax.experimental.pallas import tpu as pltpu
from jax.sharding import PartitionSpec as P

B = 64
CAP = 4
SLOTS = 64
HALF = B // 2
WIDE = 2 * B
ROWS_STEP = 8
BATCH = 4
PREP = 16
F32 = jnp.float32
BF16 = jnp.bfloat16


def left_lanes(shape):
    return lax.broadcasted_iota(jnp.int32, shape, len(shape) - 1) < B


def swap_lanes(tile):
    return jnp.concatenate([tile[:, B:], tile[:, :B]], axis=1)


def even_odd(first, second):
    left = left_lanes(first.shape)
    even = jnp.where(left, first, swap_lanes(second))
    odd = jnp.where(left, swap_lanes(first), second)
    return even, odd


def turn_pair(first, second, mixed, turned):
    even, odd = even_odd(first, second)
    mixed[pl.ds(0, HALF, stride=2)] = even
    mixed[pl.ds(1, HALF, stride=2)] = odd
    rows = mixed[...]
    turned[...] = jnp.concatenate([rows, rows], axis=0).T
    top = turned[pl.ds(0, B, stride=2)]
    low = turned[pl.ds(1, B, stride=2)]
    return jnp.where(left_lanes(top.shape), top, low)


def p_rows(p_ref, plain, turned_out, flat, mixed, turned, pair):
    for u in range(2):
        row = pair * 2 + u
        value = p_ref[row].astype(F32)
        for r in range(HALF):
            flat[u, pl.ds(2 * r, 2)] = value[:, r * WIDE : (r + 1) * WIDE]
        first = flat[u, pl.ds(0, HALF, stride=2)]
        second = flat[u, pl.ds(1, HALF, stride=2)]
        plain[row] = jnp.concatenate([first, second], axis=0).astype(BF16)
        turned_out[row] = turn_pair(first, second, mixed.at[u], turned.at[u]).astype(BF16)


def a_rows(a_ref, out, flat, pair):
    a_blocks = a_ref.shape[1]
    for u in range(2):
        row = pair * 2 + u
        value = a_ref[row].astype(F32)
        for half in range(a_blocks // 8):
            for r in range(HALF):
                flat[u, pl.ds((half * HALF + r) * 8, 8)] = value[
                    half * 8 : half * 8 + 8, r * WIDE : (r + 1) * WIDE
                ]
        for k in range(0, a_blocks, 2):
            at = (k // 8) * HALF * 8 + k % 8
            even, odd = even_odd(
                flat[u, pl.ds(at, HALF, stride=8)], flat[u, pl.ds(at + 1, HALF, stride=8)]
            )
            turned = jnp.concatenate([even, odd, even, odd], axis=0).T.astype(BF16)
            out[row * a_blocks + k] = turned[:B]
            out[row * a_blocks + k + 1] = turned[B:]


def tiles_kernel(
    p_ref, a_hbm, plain, own, low, high, a_out, flat_p, mixed, turned, flat_a, sent, got
):
    rows, a_blocks, area = a_hbm.shape
    count = lax.axis_size("dev")
    region, me = lax.axis_index("region"), lax.axis_index("dev")
    after, before = lax.rem(me + 1, count), lax.rem(me + count - 1, count)
    sides = ((after, low), (before, high))

    barrier = pltpu.get_barrier_semaphore()
    for other in (after, before):
        pl.semaphore_signal(
            barrier, inc=1, device_id=(region, other), device_id_type=pl.DeviceIdType.MESH
        )
    pl.semaphore_wait(barrier, 2)

    def halo(side, first, size):
        other, target = sides[side]
        return pltpu.make_async_remote_copy(
            src_ref=own.at[pl.ds(first, size)],
            dst_ref=target.at[pl.ds(first, size)],
            send_sem=sent.at[side],
            recv_sem=got.at[side],
            device_id=(region, other),
            device_id_type=pl.DeviceIdType.MESH,
        )

    def p_step(chunk, _):
        def one(n, _):
            p_rows(p_ref, plain, own, flat_p, mixed, turned, chunk * (PREP // 2) + n)
            return 0

        lax.fori_loop(0, PREP // 2, one, 0, unroll=4)
        for side in range(2):
            halo(side, chunk * PREP, PREP).start()
        return 0

    lax.fori_loop(0, rows // PREP, p_step, 0)

    def a_step(a_ref, out):
        def one(n, _):
            a_rows(a_ref, out, flat_a, n)
            return 0

        lax.fori_loop(0, PREP // 2, one, 0, unroll=2)

    pltpu.emit_pipeline(
        a_step,
        grid=(rows // PREP,),
        in_specs=[pl.BlockSpec((PREP, a_blocks, area), lambda i: (i, 0, 0))],
        out_specs=[pl.BlockSpec((PREP * a_blocks, B, WIDE), lambda i: (i, 0, 0))],
    )(a_hbm, a_out)

    for side in range(2):
        halo(side, 0, rows).wait()


def tiles_of(p_vals, a_vals):
    rows, a_blocks, _ = a_vals.shape
    vmem = pl.BlockSpec(memory_space=pltpu.VMEM)
    anywhere = pl.BlockSpec(memory_space=pl.ANY)
    tiles = jax.ShapeDtypeStruct((rows, B, WIDE), BF16)
    return pl.pallas_call(
        tiles_kernel,
        in_specs=[vmem, anywhere],
        out_specs=[vmem, vmem, anywhere, anywhere, anywhere],
        out_shape=[tiles] * 4 + [jax.ShapeDtypeStruct((rows * a_blocks, B, WIDE), BF16)],
        scratch_shapes=[
            pltpu.VMEM((2, B, WIDE), F32),
            pltpu.VMEM((2, B, WIDE), F32),
            pltpu.VMEM((2, WIDE, WIDE), F32),
            pltpu.VMEM((2, a_blocks * HALF, WIDE), F32),
            pltpu.SemaphoreType.DMA((2,)),
            pltpu.SemaphoreType.DMA((2,)),
        ],
        compiler_params=pltpu.CompilerParams(
            collective_id=0, has_side_effects=True, vmem_limit_bytes=48 * 2**20
        ),
        cost_estimate=pl.CostEstimate(flops=2**33, bytes_accessed=56 * 2**20, transcendentals=0),
        name="tiles",
    )(p_vals, a_vals)


def spread(tile):
    other = swap_lanes(tile)
    left = left_lanes(tile.shape)
    zero = jnp.zeros_like(tile)
    return jnp.concatenate(
        [
            jnp.where(left, tile, zero),
            jnp.where(left, other, zero),
            jnp.where(left, zero, other),
            jnp.where(left, zero, tile),
        ],
        axis=0,
    )


def terms_kernel(a_blocks, cols, slots, a_ref, p_ref, low, own, high, out, right, inner, acc0, acc1, acc2, acc3, sems):
    step = pl.program_id(0)
    rows = own.shape[0]
    shift = (lax.axis_index("dev") - 1) * rows
    accs = ((acc0, acc1), (acc2, acc3))
    copies = [
        pltpu.make_async_copy(source, right.at[pl.ds(n * rows, rows)], sems.at[n])
        for n, source in enumerate((low, own, high))
    ]

    @pl.when(step == 0)
    def _():
        for copy in copies:
            copy.start()

        def clear(n, _):
            for pair in accs:
                for acc in pair:
                    acc[n] = jnp.zeros((HALF, WIDE), F32)
            return 0

        lax.fori_loop(0, out.shape[0], clear, 0, unroll=4)
        for copy in copies:
            copy.wait()

    left = left_lanes((B, WIDE))
    zero = jnp.zeros((B, WIDE), BF16)

    def inner_tiles(row):
        fine = step * ROWS_STEP + row
        for k in range(a_blocks):
            tile = a_ref[row * a_blocks + k]
            tile = jnp.concatenate(
                [jnp.where(left, tile, zero), jnp.where(left, zero, tile)], axis=0
            )
            lhs = right[cols[k * rows + fine] - shift]
            inner[row, pl.ds(k * B, B)] = jnp.dot(
                lhs, tile, preferred_element_type=F32
            ).astype(BF16)

    def add_terms(row):
        fine = step * ROWS_STEP + row
        weights = jnp.concatenate(
            [spread(p_ref[row, pl.ds(0, HALF)]), spread(p_ref[row, pl.ds(HALF, HALF)])], axis=1
        )
        for start in range(0, a_blocks, BATCH):
            terms = jnp.dot(
                inner[row, pl.ds(start * B, BATCH * B)], weights, preferred_element_type=F32
            )
            for k in range(BATCH):
                where = [
                    [
                        slots[((q * a_blocks + start + k) * 2 + p) * rows + fine]
                        for p in range(2)
                    ]
                    for q in range(2)
                ]
                old = [[accs[q][p][where[q][p]] for p in range(2)] for q in range(2)]
                for q in range(2):
                    for p in range(2):
                        top = k * B + p * HALF
                        part = terms[top : top + HALF, q * WIDE : (q + 1) * WIDE]
                        accs[q][p][where[q][p]] = old[q][p] + part

    for row in range(ROWS_STEP):
        inner_tiles(row)
    for row in range(ROWS_STEP):
        add_terms(row)

    @pl.when(step == pl.num_programs(0) - 1)
    def _():
        def finish(n, _):
            out[n] = ((acc0[n] + acc1[n]) + (acc2[n] + acc3[n])).astype(BF16)
            return 0

        lax.fori_loop(0, out.shape[0], finish, 0, unroll=4)


def bucket_sums(a_tiles, cols, slots, p_tiles, low, own, high, buckets):
    row_total = p_tiles.shape[0]
    a_blocks = a_tiles.shape[0] // row_total
    return pl.pallas_call(
        functools.partial(terms_kernel, a_blocks),
        grid_spec=pltpu.PrefetchScalarGridSpec(
            num_scalar_prefetch=2,
            grid=(row_total // ROWS_STEP,),
            in_specs=[
                pl.BlockSpec((ROWS_STEP * a_blocks, B, WIDE), lambda i, *_: (i, 0, 0)),
                pl.BlockSpec((ROWS_STEP, B, WIDE), lambda i, *_: (i, 0, 0)),
                pl.BlockSpec(memory_space=pl.ANY),
                pl.BlockSpec(memory_space=pl.ANY),
                pl.BlockSpec(memory_space=pl.ANY),
            ],
            out_specs=pl.BlockSpec((buckets, HALF, WIDE), lambda i, *_: (0, 0, 0)),
            scratch_shapes=[pltpu.VMEM((3 * row_total, B, WIDE), BF16)]
            + [pltpu.VMEM((ROWS_STEP, a_blocks * B, WIDE), BF16)]
            + [pltpu.VMEM((buckets, HALF, WIDE), F32)] * 4
            + [pltpu.SemaphoreType.DMA((3,))],
        ),
        out_shape=jax.ShapeDtypeStruct((buckets, HALF, WIDE), BF16),
        compiler_params=pltpu.CompilerParams(
            dimension_semantics=("arbitrary",), vmem_limit_bytes=58 * 2**20
        ),
        cost_estimate=pl.CostEstimate(
            flops=2**33, bytes_accessed=24 * 2**20, transcendentals=0
        ),
        name="terms",
    )(cols, slots, a_tiles, p_tiles, low, own, high)


def owner_kernel(places, arrived, out, sums, mixed, turned, flat):
    sums[...] = jnp.zeros_like(sums)

    def add(n, _):
        place = places[n]
        sums[place] += arrived[n].astype(F32)
        return 0

    lax.fori_loop(0, arrived.shape[0], add, 0, unroll=8)

    def turn(group, _):
        for u in range(4):
            slot = group * 8 + 2 * u
            pair = turn_pair(sums[slot], sums[slot + 1], mixed.at[u], turned.at[u])
            for n in range(2):
                flat[pl.ds(2 * u + n, HALF, stride=8)] = pair[n * HALF : (n + 1) * HALF]
        for r in range(HALF):
            out[pl.ds(group * 8, 8), pl.ds(r * WIDE, WIDE)] = flat[pl.ds(r * 8, 8)]
        return 0

    lax.fori_loop(0, SLOTS // 8, turn, 0)


def owner_sums(places, arrived):
    return pl.pallas_call(
        owner_kernel,
        in_specs=[
            pl.BlockSpec(memory_space=pltpu.SMEM),
            pl.BlockSpec(memory_space=pltpu.VMEM),
        ],
        out_specs=pl.BlockSpec(memory_space=pltpu.VMEM),
        out_shape=jax.ShapeDtypeStruct((SLOTS, B * B), F32),
        scratch_shapes=[
            pltpu.VMEM((SLOTS, HALF, WIDE), F32),
            pltpu.VMEM((4, B, WIDE), F32),
            pltpu.VMEM((4, WIDE, WIDE), F32),
            pltpu.VMEM((8 * HALF, WIDE), F32),
        ],
        compiler_params=pltpu.CompilerParams(vmem_limit_bytes=32 * 2**20),
        name="owner_sums",
    )(places, arrived)


def shards(a_vals, a_cols, p_vals, send_slot, recv_slot):
    rows, a_blocks, tile_area = a_vals.shape
    owners = lax.axis_size("region") * lax.axis_size("dev")
    buckets = owners * CAP

    plain, own, low, high, a_tiles = tiles_of(p_vals, a_vals)
    cols = jnp.transpose(a_cols).reshape(-1)
    slots = jnp.transpose(send_slot, (1, 2, 3, 0)).reshape(-1)
    totals = bucket_sums(a_tiles, cols, slots, plain, low, own, high, buckets)

    arrived = lax.all_to_all(
        totals, ("region", "dev"), split_axis=0, concat_axis=0, tiled=True
    )
    return owner_sums(recv_slot.reshape(-1), arrived)


def solution(mesh):
    in_specs = (
        P(("region", "dev"), None, None),
        P(("region", "dev"), None),
        P(("region", "dev"), None, None),
        P(("region", "dev"), None, None, None),
        P(("region", "dev"), None),
    )
    out_specs = P(("region", "dev"), None)
    return jax.shard_map(shards, mesh=mesh, in_specs=in_specs, out_specs=out_specs, check_vma=False)
```

```python
import functools

import jax
import jax.numpy as jnp
from jax import lax
from jax.experimental import pallas as pl
from jax.experimental.pallas import tpu as pltpu
from jax.sharding import PartitionSpec as P

B = 64
CAP = 4
SLOTS = 64
HALF = B // 2
WIDE = 2 * B
ROWS_STEP = 8
BATCH = 4
PREP = 16
PIECES = 4
F32 = jnp.float32
BF16 = jnp.bfloat16


def left_lanes(shape):
    return lax.broadcasted_iota(jnp.int32, shape, len(shape) - 1) < B


def swap_lanes(tile):
    return jnp.concatenate([tile[:, B:], tile[:, :B]], axis=1)


def even_odd(first, second):
    left = left_lanes(first.shape)
    even = jnp.where(left, first, swap_lanes(second))
    odd = jnp.where(left, swap_lanes(first), second)
    return even, odd


def turn_pair(first, second, mixed, turned):
    even, odd = even_odd(first, second)
    mixed[pl.ds(0, HALF, stride=2)] = even
    mixed[pl.ds(1, HALF, stride=2)] = odd
    rows = mixed[...]
    turned[...] = jnp.concatenate([rows, rows], axis=0).T
    top = turned[pl.ds(0, B, stride=2)]
    low = turned[pl.ds(1, B, stride=2)]
    return jnp.where(left_lanes(top.shape), top, low)


def p_rows(p_ref, plain, turned_out, flat, mixed, turned, pair):
    for u in range(2):
        row = pair * 2 + u
        value = p_ref[row].astype(F32)
        for r in range(HALF):
            flat[u, pl.ds(2 * r, 2)] = value[:, r * WIDE : (r + 1) * WIDE]
        first = flat[u, pl.ds(0, HALF, stride=2)]
        second = flat[u, pl.ds(1, HALF, stride=2)]
        plain[row] = jnp.concatenate([first, second], axis=0).astype(BF16)
        turned_out[row] = turn_pair(first, second, mixed.at[u], turned.at[u]).astype(BF16)


def a_rows(a_ref, out, flat, pair):
    a_blocks = a_ref.shape[1]
    for u in range(2):
        row = pair * 2 + u
        value = a_ref[row].astype(F32)
        for half in range(a_blocks // 8):
            for r in range(HALF):
                flat[u, pl.ds((half * HALF + r) * 8, 8)] = value[
                    half * 8 : half * 8 + 8, r * WIDE : (r + 1) * WIDE
                ]
        for k in range(0, a_blocks, 2):
            at = (k // 8) * HALF * 8 + k % 8
            even, odd = even_odd(
                flat[u, pl.ds(at, HALF, stride=8)], flat[u, pl.ds(at + 1, HALF, stride=8)]
            )
            turned = jnp.concatenate([even, odd, even, odd], axis=0).T.astype(BF16)
            out[row * a_blocks + k] = turned[:B]
            out[row * a_blocks + k + 1] = turned[B:]


def tiles_kernel(
    p_ref, a_hbm, plain_out, own_out, low, high, a_out, plain, own, flat_p, mixed, turned,
    flat_a, sent, got, kept
):
    rows, a_blocks, area = a_hbm.shape
    count = lax.axis_size("dev")
    region, me = lax.axis_index("region"), lax.axis_index("dev")
    after, before = lax.rem(me + 1, count), lax.rem(me + count - 1, count)
    sides = ((after, low), (before, high))

    barrier = pltpu.get_barrier_semaphore()
    for other in (after, before):
        pl.semaphore_signal(
            barrier, inc=1, device_id=(region, other), device_id_type=pl.DeviceIdType.MESH
        )
    pl.semaphore_wait(barrier, 2)

    def halo(side, first, size):
        other, target = sides[side]
        return pltpu.make_async_remote_copy(
            src_ref=own.at[pl.ds(first, size)],
            dst_ref=target.at[pl.ds(first, size)],
            send_sem=sent.at[side],
            recv_sem=got.at[side],
            device_id=(region, other),
            device_id_type=pl.DeviceIdType.MESH,
        )

    def keep(which, first, size):
        source, target = ((plain, plain_out), (own, own_out))[which]
        return pltpu.make_async_copy(
            source.at[pl.ds(first, size)], target.at[pl.ds(first, size)], kept.at[which]
        )

    def p_step(chunk, _):
        def one(n, _):
            p_rows(p_ref, plain, own, flat_p, mixed, turned, chunk * (PREP // 2) + n)
            return 0

        lax.fori_loop(0, PREP // 2, one, 0, unroll=4)
        for side in range(2):
            halo(side, chunk * PREP, PREP).start()
            keep(side, chunk * PREP, PREP).start()
        return 0

    lax.fori_loop(0, rows // PREP, p_step, 0)

    def a_step(a_ref, out):
        def one(n, _):
            a_rows(a_ref, out, flat_a, n)
            return 0

        lax.fori_loop(0, PREP // 2, one, 0, unroll=2)

    pltpu.emit_pipeline(
        a_step,
        grid=(rows // PREP,),
        in_specs=[pl.BlockSpec((PREP, a_blocks, area), lambda i: (i, 0, 0))],
        out_specs=[pl.BlockSpec((PREP * a_blocks, B, WIDE), lambda i: (i, 0, 0))],
    )(a_hbm, a_out)

    for side in range(2):
        keep(side, 0, rows).wait()
        halo(side, 0, rows).wait()


def tiles_of(p_vals, a_vals):
    rows, a_blocks, _ = a_vals.shape
    vmem = pl.BlockSpec(memory_space=pltpu.VMEM)
    anywhere = pl.BlockSpec(memory_space=pl.ANY)
    tiles = jax.ShapeDtypeStruct((rows, B, WIDE), BF16)
    return pl.pallas_call(
        tiles_kernel,
        in_specs=[vmem, anywhere],
        out_specs=[pl.BlockSpec(memory_space=pltpu.HBM)] * 5,
        out_shape=[tiles] * 4 + [jax.ShapeDtypeStruct((rows * a_blocks, B, WIDE), BF16)],
        scratch_shapes=[
            pltpu.VMEM((rows, B, WIDE), BF16),
            pltpu.VMEM((rows, B, WIDE), BF16),
            pltpu.VMEM((2, B, WIDE), F32),
            pltpu.VMEM((2, B, WIDE), F32),
            pltpu.VMEM((2, WIDE, WIDE), F32),
            pltpu.VMEM((2, a_blocks * HALF, WIDE), F32),
            pltpu.SemaphoreType.DMA((2,)),
            pltpu.SemaphoreType.DMA((2,)),
            pltpu.SemaphoreType.DMA((2,)),
        ],
        compiler_params=pltpu.CompilerParams(
            collective_id=0, has_side_effects=True, vmem_limit_bytes=62 * 2**20
        ),
        cost_estimate=pl.CostEstimate(flops=2**33, bytes_accessed=56 * 2**20, transcendentals=0),
        name="tiles",
    )(p_vals, a_vals)


def spread(tile):
    other = swap_lanes(tile)
    left = left_lanes(tile.shape)
    zero = jnp.zeros_like(tile)
    return jnp.concatenate(
        [
            jnp.where(left, tile, zero),
            jnp.where(left, other, zero),
            jnp.where(left, zero, other),
            jnp.where(left, zero, tile),
        ],
        axis=0,
    )


def terms_kernel(a_blocks, cols, slots, a_ref, p_ref, low, own, high, out, right, inner, done, acc0, acc1, acc2, acc3, sems):
    step = pl.program_id(0)
    rows = own.shape[0]
    shift = (lax.axis_index("dev") - 1) * rows
    accs = ((acc0, acc1), (acc2, acc3))
    copies = [
        pltpu.make_async_copy(source, right.at[pl.ds(n * rows, rows)], sems.at[n])
        for n, source in enumerate((low, own, high))
    ]

    @pl.when(step == 0)
    def _():
        for copy in copies:
            copy.start()

        def clear(n, _):
            for pair in accs:
                for acc in pair:
                    acc[n] = jnp.zeros((HALF, WIDE), F32)
            return 0

        lax.fori_loop(0, done.shape[0], clear, 0, unroll=4)
        for copy in copies:
            copy.wait()

    left = left_lanes((B, WIDE))
    zero = jnp.zeros((B, WIDE), BF16)

    def inner_tiles(row):
        fine = step * ROWS_STEP + row
        for k in range(a_blocks):
            tile = a_ref[row * a_blocks + k]
            tile = jnp.concatenate(
                [jnp.where(left, tile, zero), jnp.where(left, zero, tile)], axis=0
            )
            lhs = right[cols[k * rows + fine] - shift]
            inner[row, pl.ds(k * B, B)] = jnp.dot(
                lhs, tile, preferred_element_type=F32
            ).astype(BF16)

    def add_terms(row):
        fine = step * ROWS_STEP + row
        weights = jnp.concatenate(
            [spread(p_ref[row, pl.ds(0, HALF)]), spread(p_ref[row, pl.ds(HALF, HALF)])], axis=1
        )
        for start in range(0, a_blocks, BATCH):
            terms = jnp.dot(
                inner[row, pl.ds(start * B, BATCH * B)], weights, preferred_element_type=F32
            )
            for k in range(BATCH):
                where = [
                    [
                        slots[((q * a_blocks + start + k) * 2 + p) * rows + fine]
                        for p in range(2)
                    ]
                    for q in range(2)
                ]
                old = [[accs[q][p][where[q][p]] for p in range(2)] for q in range(2)]
                for q in range(2):
                    for p in range(2):
                        top = k * B + p * HALF
                        part = terms[top : top + HALF, q * WIDE : (q + 1) * WIDE]
                        accs[q][p][where[q][p]] = old[q][p] + part

    for row in range(ROWS_STEP):
        inner_tiles(row)
    for row in range(ROWS_STEP):
        add_terms(row)

    @pl.when(step == pl.num_programs(0) - 1)
    def _():
        leaving = []
        for piece in range(PIECES):
            size = done.shape[0] // PIECES

            def finish(n, _):
                n = piece * size + n
                done[n] = ((acc0[n] + acc1[n]) + (acc2[n] + acc3[n])).astype(BF16)
                return 0

            lax.fori_loop(0, size, finish, 0, unroll=4)
            part = pl.ds(piece * size, size)
            copy = pltpu.make_async_copy(done.at[part], out.at[part], sems.at[3 + piece])
            copy.start()
            leaving.append(copy)
        for copy in leaving:
            copy.wait()


def bucket_sums(a_tiles, cols, slots, p_tiles, low, own, high, buckets):
    row_total = p_tiles.shape[0]
    a_blocks = a_tiles.shape[0] // row_total
    return pl.pallas_call(
        functools.partial(terms_kernel, a_blocks),
        grid_spec=pltpu.PrefetchScalarGridSpec(
            num_scalar_prefetch=2,
            grid=(row_total // ROWS_STEP,),
            in_specs=[
                pl.BlockSpec((ROWS_STEP * a_blocks, B, WIDE), lambda i, *_: (i, 0, 0)),
                pl.BlockSpec((ROWS_STEP, B, WIDE), lambda i, *_: (i, 0, 0)),
                pl.BlockSpec(memory_space=pl.ANY),
                pl.BlockSpec(memory_space=pl.ANY),
                pl.BlockSpec(memory_space=pl.ANY),
            ],
            out_specs=pl.BlockSpec(memory_space=pl.ANY),
            scratch_shapes=[pltpu.VMEM((3 * row_total, B, WIDE), BF16)]
            + [pltpu.VMEM((ROWS_STEP, a_blocks * B, WIDE), BF16)]
            + [pltpu.VMEM((buckets, HALF, WIDE), BF16)]
            + [pltpu.VMEM((buckets, HALF, WIDE), F32)] * 4
            + [pltpu.SemaphoreType.DMA((3 + PIECES,))],
        ),
        out_shape=jax.ShapeDtypeStruct((buckets, HALF, WIDE), BF16),
        compiler_params=pltpu.CompilerParams(
            dimension_semantics=("arbitrary",), vmem_limit_bytes=58 * 2**20
        ),
        cost_estimate=pl.CostEstimate(
            flops=2**33, bytes_accessed=24 * 2**20, transcendentals=0
        ),
        name="terms",
    )(cols, slots, a_tiles, p_tiles, low, own, high)


def owner_kernel(places, arrived, out, sum0, sum1, sum2, sum3, mixed, turned, flat):
    sums = (sum0, sum1, sum2, sum3)
    for part in sums:
        part[...] = jnp.zeros_like(part)

    def add(n, _):
        at = [places[4 * n + u] for u in range(4)]
        old = [sums[u][at[u]] for u in range(4)]
        for u in range(4):
            sums[u][at[u]] = old[u] + arrived[4 * n + u].astype(F32)
        return 0

    lax.fori_loop(0, arrived.shape[0] // 4, add, 0, unroll=4)

    def total(slot):
        return (sum0[slot] + sum1[slot]) + (sum2[slot] + sum3[slot])

    def turn(group, _):
        for u in range(4):
            slot = group * 8 + 2 * u
            pair = turn_pair(total(slot), total(slot + 1), mixed.at[u], turned.at[u])
            for n in range(2):
                flat[pl.ds(2 * u + n, HALF, stride=8)] = pair[n * HALF : (n + 1) * HALF]
        for r in range(HALF):
            out[pl.ds(group * 8, 8), pl.ds(r * WIDE, WIDE)] = flat[pl.ds(r * 8, 8)]
        return 0

    lax.fori_loop(0, SLOTS // 8, turn, 0)


def owner_sums(places, arrived):
    return pl.pallas_call(
        owner_kernel,
        in_specs=[
            pl.BlockSpec(memory_space=pltpu.SMEM),
            pl.BlockSpec(memory_space=pltpu.VMEM),
        ],
        out_specs=pl.BlockSpec(memory_space=pltpu.VMEM),
        out_shape=jax.ShapeDtypeStruct((SLOTS, B * B), F32),
        scratch_shapes=[
            *[pltpu.VMEM((SLOTS, HALF, WIDE), F32)] * 4,
            pltpu.VMEM((4, B, WIDE), F32),
            pltpu.VMEM((4, WIDE, WIDE), F32),
            pltpu.VMEM((8 * HALF, WIDE), F32),
        ],
        compiler_params=pltpu.CompilerParams(vmem_limit_bytes=32 * 2**20),
        name="owner_sums",
    )(places, arrived)


def shards(a_vals, a_cols, p_vals, send_slot, recv_slot):
    rows, a_blocks, tile_area = a_vals.shape
    owners = lax.axis_size("region") * lax.axis_size("dev")
    buckets = owners * CAP

    plain, own, low, high, a_tiles = tiles_of(p_vals, a_vals)
    cols = jnp.transpose(a_cols).reshape(-1)
    slots = jnp.transpose(send_slot, (1, 2, 3, 0)).reshape(-1)
    totals = bucket_sums(a_tiles, cols, slots, plain, low, own, high, buckets)

    arrived = lax.all_to_all(
        totals, ("region", "dev"), split_axis=0, concat_axis=0, tiled=True
    )
    return owner_sums(recv_slot.reshape(-1), arrived)


def solution(mesh):
    in_specs = (
        P(("region", "dev"), None, None),
        P(("region", "dev"), None),
        P(("region", "dev"), None, None),
        P(("region", "dev"), None, None, None),
        P(("region", "dev"), None),
    )
    out_specs = P(("region", "dev"), None)
    return jax.shard_map(shards, mesh=mesh, in_specs=in_specs, out_specs=out_specs, check_vma=False)
```

```python
import functools

import jax
import jax.numpy as jnp
from jax import lax
from jax.experimental import pallas as pl
from jax.experimental.pallas import tpu as pltpu
from jax.sharding import PartitionSpec as P

B = 64
CAP = 4
SLOTS = 64
HALF = B // 2
WIDE = 2 * B
ROWS_STEP = 8
BATCH = 4
PREP = 16
A_STEP = 8
PIECES = 4
F32 = jnp.float32
BF16 = jnp.bfloat16


def left_lanes(shape):
    return lax.broadcasted_iota(jnp.int32, shape, len(shape) - 1) < B


def swap_lanes(tile):
    return jnp.concatenate([tile[:, B:], tile[:, :B]], axis=1)


def even_odd(first, second):
    left = left_lanes(first.shape)
    even = jnp.where(left, first, swap_lanes(second))
    odd = jnp.where(left, swap_lanes(first), second)
    return even, odd


def turn_pair(first, second, mixed, turned):
    even, odd = even_odd(first, second)
    mixed[pl.ds(0, HALF, stride=2)] = even
    mixed[pl.ds(1, HALF, stride=2)] = odd
    rows = mixed[...]
    turned[...] = jnp.concatenate([rows, rows], axis=0).T
    top = turned[pl.ds(0, B, stride=2)]
    low = turned[pl.ds(1, B, stride=2)]
    return jnp.where(left_lanes(top.shape), top, low)


def p_rows(p_ref, plain, turned_out, flat, mixed, turned, pair):
    for u in range(2):
        row = pair * 2 + u
        value = p_ref[row].astype(F32)
        for r in range(HALF):
            flat[u, pl.ds(2 * r, 2)] = value[:, r * WIDE : (r + 1) * WIDE]
        first = flat[u, pl.ds(0, HALF, stride=2)]
        second = flat[u, pl.ds(1, HALF, stride=2)]
        plain[row] = jnp.concatenate([first, second], axis=0).astype(BF16)
        turned_out[row] = turn_pair(first, second, mixed.at[u], turned.at[u]).astype(BF16)


def a_rows(a_ref, out, flat, pair):
    a_blocks = a_ref.shape[1]
    for u in range(2):
        row = pair * 2 + u
        value = a_ref[row].astype(F32)
        for half in range(a_blocks // 8):
            for r in range(HALF):
                flat[u, pl.ds((half * HALF + r) * 8, 8)] = value[
                    half * 8 : half * 8 + 8, r * WIDE : (r + 1) * WIDE
                ]
        for k in range(0, a_blocks, 2):
            at = (k // 8) * HALF * 8 + k % 8
            even, odd = even_odd(
                flat[u, pl.ds(at, HALF, stride=8)], flat[u, pl.ds(at + 1, HALF, stride=8)]
            )
            turned = jnp.concatenate([even, odd, even, odd], axis=0).T.astype(BF16)
            out[row * a_blocks + k] = turned[:B]
            out[row * a_blocks + k + 1] = turned[B:]


def tiles_kernel(
    p_ref, a_hbm, plain_out, own_out, low, high, a_out, plain, own, flat_p, mixed, turned,
    flat_a, sent, got, kept
):
    rows, a_blocks, area = a_hbm.shape
    count = lax.axis_size("dev")
    region, me = lax.axis_index("region"), lax.axis_index("dev")
    after, before = lax.rem(me + 1, count), lax.rem(me + count - 1, count)
    sides = ((after, low), (before, high))

    barrier = pltpu.get_barrier_semaphore()
    for other in (after, before):
        pl.semaphore_signal(
            barrier, inc=1, device_id=(region, other), device_id_type=pl.DeviceIdType.MESH
        )
    pl.semaphore_wait(barrier, 2)

    def halo(side, first, size):
        other, target = sides[side]
        return pltpu.make_async_remote_copy(
            src_ref=own.at[pl.ds(first, size)],
            dst_ref=target.at[pl.ds(first, size)],
            send_sem=sent.at[side],
            recv_sem=got.at[side],
            device_id=(region, other),
            device_id_type=pl.DeviceIdType.MESH,
        )

    def keep(which, first, size):
        source, target = ((plain, plain_out), (own, own_out))[which]
        return pltpu.make_async_copy(
            source.at[pl.ds(first, size)], target.at[pl.ds(first, size)], kept.at[which]
        )

    def p_step(chunk, _):
        def one(n, _):
            p_rows(p_ref, plain, own, flat_p, mixed, turned, chunk * (PREP // 2) + n)
            return 0

        lax.fori_loop(0, PREP // 2, one, 0, unroll=4)
        for side in range(2):
            halo(side, chunk * PREP, PREP).start()
            keep(side, chunk * PREP, PREP).start()
        return 0

    lax.fori_loop(0, rows // PREP, p_step, 0)

    def a_step(a_ref, out):
        def one(n, _):
            a_rows(a_ref, out, flat_a, n)
            return 0

        lax.fori_loop(0, A_STEP // 2, one, 0, unroll=2)

    pltpu.emit_pipeline(
        a_step,
        grid=(rows // A_STEP,),
        in_specs=[pl.BlockSpec((A_STEP, a_blocks, area), lambda i: (i, 0, 0))],
        out_specs=[pl.BlockSpec((A_STEP * a_blocks, B, WIDE), lambda i: (i, 0, 0))],
    )(a_hbm, a_out)

    for side in range(2):
        keep(side, 0, rows).wait()
        halo(side, 0, rows).wait()


def tiles_of(p_vals, a_vals):
    rows, a_blocks, _ = a_vals.shape
    vmem = pl.BlockSpec(memory_space=pltpu.VMEM)
    anywhere = pl.BlockSpec(memory_space=pl.ANY)
    tiles = jax.ShapeDtypeStruct((rows, B, WIDE), BF16)
    return pl.pallas_call(
        tiles_kernel,
        in_specs=[vmem, anywhere],
        out_specs=[pl.BlockSpec(memory_space=pltpu.HBM)] * 5,
        out_shape=[tiles] * 4 + [jax.ShapeDtypeStruct((rows * a_blocks, B, WIDE), BF16)],
        scratch_shapes=[
            pltpu.VMEM((rows, B, WIDE), BF16),
            pltpu.VMEM((rows, B, WIDE), BF16),
            pltpu.VMEM((2, B, WIDE), F32),
            pltpu.VMEM((2, B, WIDE), F32),
            pltpu.VMEM((2, WIDE, WIDE), F32),
            pltpu.VMEM((2, a_blocks * HALF, WIDE), F32),
            pltpu.SemaphoreType.DMA((2,)),
            pltpu.SemaphoreType.DMA((2,)),
            pltpu.SemaphoreType.DMA((2,)),
        ],
        compiler_params=pltpu.CompilerParams(
            collective_id=0, has_side_effects=True, vmem_limit_bytes=62 * 2**20
        ),
        cost_estimate=pl.CostEstimate(flops=2**33, bytes_accessed=56 * 2**20, transcendentals=0),
        name="tiles",
    )(p_vals, a_vals)


def spread(tile):
    other = swap_lanes(tile)
    left = left_lanes(tile.shape)
    zero = jnp.zeros_like(tile)
    return jnp.concatenate(
        [
            jnp.where(left, tile, zero),
            jnp.where(left, other, zero),
            jnp.where(left, zero, other),
            jnp.where(left, zero, tile),
        ],
        axis=0,
    )


def terms_kernel(a_blocks, cols, slots, a_ref, p_ref, low, own, high, out, right, inner, done, acc0, acc1, acc2, acc3, sems):
    step = pl.program_id(0)
    rows = own.shape[0]
    shift = (lax.axis_index("dev") - 1) * rows
    accs = ((acc0, acc1), (acc2, acc3))
    copies = [
        pltpu.make_async_copy(source, right.at[pl.ds(n * rows, rows)], sems.at[n])
        for n, source in enumerate((low, own, high))
    ]

    @pl.when(step == 0)
    def _():
        for copy in copies:
            copy.start()

        def clear(n, _):
            for pair in accs:
                for acc in pair:
                    acc[n] = jnp.zeros((HALF, WIDE), F32)
            return 0

        lax.fori_loop(0, done.shape[0], clear, 0, unroll=8)
        for copy in copies:
            copy.wait()

    left = left_lanes((B, WIDE))
    zero = jnp.zeros((B, WIDE), BF16)

    def inner_tiles(row):
        fine = step * ROWS_STEP + row
        for k in range(a_blocks):
            tile = a_ref[row * a_blocks + k]
            tile = jnp.concatenate(
                [jnp.where(left, tile, zero), jnp.where(left, zero, tile)], axis=0
            )
            lhs = right[cols[k * rows + fine] - shift]
            inner[row, pl.ds(k * B, B)] = jnp.dot(
                lhs, tile, preferred_element_type=F32
            ).astype(BF16)

    def add_terms(row):
        fine = step * ROWS_STEP + row
        weights = jnp.concatenate(
            [spread(p_ref[row, pl.ds(0, HALF)]), spread(p_ref[row, pl.ds(HALF, HALF)])], axis=1
        )
        for start in range(0, a_blocks, BATCH):
            terms = jnp.dot(
                inner[row, pl.ds(start * B, BATCH * B)], weights, preferred_element_type=F32
            )
            for k in range(BATCH):
                where = [
                    [
                        slots[((q * a_blocks + start + k) * 2 + p) * rows + fine]
                        for p in range(2)
                    ]
                    for q in range(2)
                ]
                old = [[accs[q][p][where[q][p]] for p in range(2)] for q in range(2)]
                for q in range(2):
                    for p in range(2):
                        top = k * B + p * HALF
                        part = terms[top : top + HALF, q * WIDE : (q + 1) * WIDE]
                        accs[q][p][where[q][p]] = old[q][p] + part

    for row in range(ROWS_STEP):
        inner_tiles(row)
    for row in range(ROWS_STEP):
        add_terms(row)

    @pl.when(step == pl.num_programs(0) - 1)
    def _():
        leaving = []
        for piece in range(PIECES):
            size = done.shape[0] // PIECES

            def finish(n, _):
                n = piece * size + n
                done[n] = ((acc0[n] + acc1[n]) + (acc2[n] + acc3[n])).astype(BF16)
                return 0

            lax.fori_loop(0, size, finish, 0, unroll=8)
            part = pl.ds(piece * size, size)
            copy = pltpu.make_async_copy(done.at[part], out.at[part], sems.at[3 + piece])
            copy.start()
            leaving.append(copy)
        for copy in leaving:
            copy.wait()


def bucket_sums(a_tiles, cols, slots, p_tiles, low, own, high, buckets):
    row_total = p_tiles.shape[0]
    a_blocks = a_tiles.shape[0] // row_total
    return pl.pallas_call(
        functools.partial(terms_kernel, a_blocks),
        grid_spec=pltpu.PrefetchScalarGridSpec(
            num_scalar_prefetch=2,
            grid=(row_total // ROWS_STEP,),
            in_specs=[
                pl.BlockSpec((ROWS_STEP * a_blocks, B, WIDE), lambda i, *_: (i, 0, 0)),
                pl.BlockSpec((ROWS_STEP, B, WIDE), lambda i, *_: (i, 0, 0)),
                pl.BlockSpec(memory_space=pl.ANY),
                pl.BlockSpec(memory_space=pl.ANY),
                pl.BlockSpec(memory_space=pl.ANY),
            ],
            out_specs=pl.BlockSpec(memory_space=pl.ANY),
            scratch_shapes=[pltpu.VMEM((3 * row_total, B, WIDE), BF16)]
            + [pltpu.VMEM((ROWS_STEP, a_blocks * B, WIDE), BF16)]
            + [pltpu.VMEM((buckets, HALF, WIDE), BF16)]
            + [pltpu.VMEM((buckets, HALF, WIDE), F32)] * 4
            + [pltpu.SemaphoreType.DMA((3 + PIECES,))],
        ),
        out_shape=jax.ShapeDtypeStruct((buckets, HALF, WIDE), BF16),
        compiler_params=pltpu.CompilerParams(
            dimension_semantics=("arbitrary",), vmem_limit_bytes=58 * 2**20
        ),
        cost_estimate=pl.CostEstimate(
            flops=2**33, bytes_accessed=24 * 2**20, transcendentals=0
        ),
        name="terms",
    )(cols, slots, a_tiles, p_tiles, low, own, high)


def owner_kernel(places, arrived, out, sum0, sum1, sum2, sum3, mixed, turned, flat):
    sums = (sum0, sum1, sum2, sum3)
    for part in sums:
        part[...] = jnp.zeros_like(part)

    def add(n, _):
        at = [places[4 * n + u] for u in range(4)]
        old = [sums[u][at[u]] for u in range(4)]
        for u in range(4):
            sums[u][at[u]] = old[u] + arrived[4 * n + u].astype(F32)
        return 0

    lax.fori_loop(0, arrived.shape[0] // 4, add, 0, unroll=4)

    def total(slot):
        return (sum0[slot] + sum1[slot]) + (sum2[slot] + sum3[slot])

    def turn(group, _):
        for u in range(4):
            slot = group * 8 + 2 * u
            pair = turn_pair(total(slot), total(slot + 1), mixed.at[u], turned.at[u])
            for n in range(2):
                flat[pl.ds(2 * u + n, HALF, stride=8)] = pair[n * HALF : (n + 1) * HALF]
        for r in range(HALF):
            out[pl.ds(group * 8, 8), pl.ds(r * WIDE, WIDE)] = flat[pl.ds(r * 8, 8)]
        return 0

    lax.fori_loop(0, SLOTS // 8, turn, 0)


def owner_sums(places, arrived):
    return pl.pallas_call(
        owner_kernel,
        in_specs=[
            pl.BlockSpec(memory_space=pltpu.SMEM),
            pl.BlockSpec(memory_space=pltpu.VMEM),
        ],
        out_specs=pl.BlockSpec(memory_space=pltpu.VMEM),
        out_shape=jax.ShapeDtypeStruct((SLOTS, B * B), F32),
        scratch_shapes=[
            *[pltpu.VMEM((SLOTS, HALF, WIDE), F32)] * 4,
            pltpu.VMEM((4, B, WIDE), F32),
            pltpu.VMEM((4, WIDE, WIDE), F32),
            pltpu.VMEM((8 * HALF, WIDE), F32),
        ],
        compiler_params=pltpu.CompilerParams(vmem_limit_bytes=32 * 2**20),
        name="owner_sums",
    )(places, arrived)


def shards(a_vals, a_cols, p_vals, send_slot, recv_slot):
    rows, a_blocks, tile_area = a_vals.shape
    owners = lax.axis_size("region") * lax.axis_size("dev")
    buckets = owners * CAP

    plain, own, low, high, a_tiles = tiles_of(p_vals, a_vals)
    cols = jnp.transpose(a_cols).reshape(-1)
    slots = jnp.transpose(send_slot, (1, 2, 3, 0)).reshape(-1)
    totals = bucket_sums(a_tiles, cols, slots, plain, low, own, high, buckets)

    arrived = lax.all_to_all(
        totals, ("region", "dev"), split_axis=0, concat_axis=0, tiled=True
    )
    return owner_sums(recv_slot.reshape(-1), arrived)


def solution(mesh):
    in_specs = (
        P(("region", "dev"), None, None),
        P(("region", "dev"), None),
        P(("region", "dev"), None, None),
        P(("region", "dev"), None, None, None),
        P(("region", "dev"), None),
    )
    out_specs = P(("region", "dev"), None)
    return jax.shard_map(shards, mesh=mesh, in_specs=in_specs, out_specs=out_specs, check_vma=False)
```
